256 devices in a mesh: row: 16 (over y_hi, z), col: 16 (over x, y_lo, core).
Axes of the slice: x: 4, y: 4 (y_hi: 2, y_lo: 2; y = y_hi * 2 + y_lo), z: 8, core: 2. Of those that a mesh axis runs over, the one named last changes fastest.
Arguments:
- covariance: bfloat16 [8192, 131072], P('row', 'col'), may hold values from -6 to 6
- operator_rows: bfloat16 [512, 131072], P('row', 'col'), may hold values from -0.015625 to 0.015625
- row_index: int32 [512], replicated, may hold values from 0 to 511, each once
Outputs:
- cross_cov: bfloat16 [8192, 512], P(('row', 'col'))
The draws below stay inside these ranges and needn't reach their ends.
Inputs may be any that keep to these rules, and one draw needn't show every extreme that they name: `row_index`: each stored row is named by exactly one observation.
All inputs are finite; a program needn't handle non-finite values.
Results may differ from the reference program's by a relative error of at most 0.0015.
Values may be sent and summed in bfloat16 or wider, within the bound.
No kernel may reach another device: no remote copies, remote signals or barrier semaphores. Data moves between devices by JAX's collectives and lax.ppermute only.
A program may use at most 64 MiB of HBM per device.

```python
import jax
import jax.numpy as jnp
from jax import lax

K = 131072
M = 64
NPAN = 8
ROWS_DEV = 512
OBS = 512
ROWS = 8192
N_ROW = 16


def raised(values, own_key, source, target, blocks, factor):
    owner, partner = [(jnp.arange(values.shape[dim]) // (values.shape[dim] // blocks)).reshape([-1 if axis == dim else 1 for axis in range(values.ndim)]) for dim in (source, target)]
    chosen = jax.random.permutation(own_key, blocks)[partner]
    strong = (owner == chosen) | (owner == (partner + blocks // 2) % blocks)
    return jnp.where(strong, factor * values, values)


def block_levels(key, shape, cuts, low, top_value):
    level, own = 1.0, jax.random.fold_in(key, 6)
    for dim, parts in cuts:
        steps = jnp.exp(jax.random.uniform(jax.random.fold_in(own, dim), (parts,), jnp.float32, low / len(cuts), top_value / len(cuts)))
        level = level * jnp.repeat(steps, shape[dim] // parts).reshape([-1 if axis == dim else 1 for axis in range(len(shape))])
    return level


def gaussian(rng, dims, spread, most, pieces=(), kind=jnp.bfloat16):
    entries = spread * jax.random.normal(rng, dims, jnp.float32)
    if pieces:
        entries = entries * block_levels(rng, dims, pieces, -0.22, 0.18)
    return jnp.clip(entries, -most, most).astype(kind)


def bell_draw_with(rng, extent, scale, most, pieces, heavy, held_as=jnp.bfloat16):
    drawn = scale * jax.random.normal(rng, extent, jnp.float32)
    if pieces:
        drawn = drawn * block_levels(rng, extent, pieces, -0.22, 0.18)
    return jnp.clip(raised(drawn, jax.random.fold_in(rng, 3), *heavy), -most, most).astype(held_as)


def setup_inputs(seed: int = 0) -> dict:
    streams_of = jax.random.split(jax.random.key(seed), 4)
    return {
        "covariance": bell_draw_with(streams_of[0], (ROWS, K), 1.0, 6.0, ((0, 16), (1, 16)), (1, 0, 16, 2.0)),
        "operator_rows": gaussian(streams_of[1], (OBS, K), K ** -0.5, 0.015625, ((0, 16), (1, 16))),
        "row_index": jax.random.permutation(streams_of[2], OBS).astype(jnp.int32),
    }


def reference(covariance, operator_rows, row_index):
    selected = jnp.take(operator_rows, row_index.astype(jnp.int32), axis=0)
    flipped = selected.T
    blocks = covariance.reshape(N_ROW, ROWS_DEV, K)

    def one_block(block):
        return jnp.dot(block, flipped, preferred_element_type=jnp.float32).astype(jnp.bfloat16)

    result = lax.map(one_block, blocks)
    return result.reshape(ROWS_DEV * N_ROW, NPAN * M)
```

```python
import functools

import jax
import jax.numpy as jnp
import numpy as np
from jax import lax
from jax.experimental import pallas as pl
from jax.experimental.pallas import tpu as pltpu
from jax.sharding import PartitionSpec as P

BOTH = ("row", "col")
XS, YS, ZS, CORES = 4, 4, 8, 2
UNIT = 16
STEP_K = 1024


def index_of(x, y, z, core):
    return ((y // 2) * ZS + z) * 16 + x * 4 + (y % 2) * 2 + core


def moved(values, target):
    pairs = []
    for place in np.ndindex(XS, YS, ZS, CORES):
        x, y, z, core = target(*place)
        pairs.append((index_of(*place), index_of(x % XS, y % YS, z % ZS, core)))
    return lax.ppermute(values, BOTH, pairs)


def ahead(x, y, z, core):
    return x, y, z + 1 - 2 * core, core


def behind(x, y, z, core):
    return x, y, z - 1 + 2 * core, core


def across(x, y, z, core):
    return x, y + 2, z, core


def other_core(x, y, z, core):
    return x, y, z, 1 - core


GROUPS = (
    tuple((0, u) for u in "ABPQ") + ((1, "A"), (-1, "A"), (1, "B"), (-1, "B")),
    ((1, "P"), (-1, "P"), (1, "Q"), (-1, "Q"), (2, "A"), (-2, "A"), (2, "B"), (-2, "B")),
    ((2, "P"), (-2, "P"), (2, "Q"), (-2, "Q"), (3, "A"), (-3, "A"), (3, "B"), (-3, "B")),
    ((3, "P"), (-3, "P"), (3, "Q"), (-3, "Q")) + tuple((4, u) for u in "ABPQ"),
)


def product_kernel(slots, core_ref, cov_ref, *refs):
    chunks, (keep_ref, send_ref, total) = refs[: len(slots)], refs[len(slots) :]
    step = pl.program_id(0)
    core = core_ref[0]
    at = {slot: n for n, slot in enumerate(slots)}
    rows = []
    for n, (k, unit) in enumerate(slots):
        if k in (0, 4):
            rows.append(chunks[n][...])
        else:
            rows.append(jnp.where(core == 0, chunks[n][...], chunks[at[-k, unit]][...]))
    part = lax.dot_general(
        cov_ref[...], jnp.concatenate(rows, 0), (((1,), (1,)), ((), ())),
        preferred_element_type=jnp.float32,
    )

    @pl.when(step == 0)
    def _():
        total[...] = part

    @pl.when(step > 0)
    def _():
        total[...] += part

    @pl.when(step == pl.num_programs(0) - 1)
    def _():
        for n in range(8):
            here = pl.ds(n * 32, 32)
            keep_ref[here, :] = total[pl.ds((2 * n + core) * 32, 32), :]
            send_ref[here, :] = total[pl.ds((2 * n + 1 - core) * 32, 32), :]


def product(core, covariance, slots, chunks):
    height, depth = covariance.shape
    width = UNIT * len(slots)
    half = jax.ShapeDtypeStruct((height // 2, width), jnp.float32)
    whole = pl.BlockSpec((height // 2, width), lambda i: (0, 0))
    return pl.pallas_call(
        functools.partial(product_kernel, slots),
        grid=(depth // STEP_K,),
        in_specs=[pl.BlockSpec(memory_space=pltpu.SMEM), pl.BlockSpec((height, STEP_K), lambda i: (0, i))]
        + [pl.BlockSpec((UNIT, STEP_K), lambda i: (0, i))] * len(slots),
        out_specs=[whole, whole],
        out_shape=[half, half],
        scratch_shapes=[pltpu.VMEM((height, width), jnp.float32)],
        compiler_params=pltpu.CompilerParams(vmem_limit_bytes=16 * 1024 * 1024),
        cost_estimate=pl.CostEstimate(
            flops=2 * height * width * depth,
            bytes_accessed=2 * depth * (height + width),
            transcendentals=0,
        ),
    )(core, covariance, *chunks)


def on_device(covariance, operator_rows, row_index):
    row, col = lax.axis_index("row"), lax.axis_index("col")
    core = col % 2
    got = {(0, "A"): operator_rows[:UNIT], (0, "B"): operator_rows[UNIT:]}
    got[0, "P"] = moved(got[0, "A"], across)
    got[0, "Q"] = moved(got[0, "B"], across)
    for k in (1, 2, 3, 4):
        for unit in "BAP":
            got[k, unit] = moved(got[k - 1, unit], ahead)
            if k < 4:
                got[-k, unit] = moved(got[1 - k, unit], behind)
            if unit == "B":
                got[k, "Q"] = moved(got[k, "B"], across)
                if k < 4:
                    got[-k, "Q"] = moved(got[-k, "B"], across)

    core_of = jnp.full((1,), core, jnp.int32)
    keeps, sends = zip(*(product(core_of, covariance, g, [got[s] for s in g]) for g in GROUPS))
    came = moved(jnp.concatenate(sends, 1), other_core)
    sums = (jnp.concatenate(keeps, 1) + came).reshape(8, 32, -1)
    groups = [[2 * n + c for n in range(8)] for c in range(2)]
    summed = lax.all_to_all(sums, "col", 0, 0, axis_index_groups=groups).sum(0)

    slots = [s for g in GROUPS for s in g]
    shift = np.repeat([-k for k, _ in slots], UNIT)
    far = np.repeat([u in "PQ" for _, u in slots], UNIT).astype(np.int32)
    first = np.repeat([UNIT * (u in "BQ") for _, u in slots], UNIT) + np.tile(np.arange(UNIT), len(slots))
    y_hi, z = row // ZS, row % ZS
    stored = (((y_hi + far) % 2) * ZS + (z + shift) % ZS) * (2 * UNIT) + first
    places = (stored[:, None] == row_index[None, :]).astype(jnp.bfloat16)
    ordered = jnp.dot(summed.astype(jnp.bfloat16), places, preferred_element_type=jnp.float32)
    return ordered.astype(jnp.bfloat16)


def solution(mesh):
    in_specs = (P("row", "col"), P("row", "col"), P())
    out_specs = P(BOTH, None)
    return jax.shard_map(on_device, mesh=mesh, in_specs=in_specs, out_specs=out_specs, check_vma=False)
```

```python
import functools

import jax
import jax.numpy as jnp
import numpy as np
from jax import lax
from jax.experimental import pallas as pl
from jax.experimental.pallas import tpu as pltpu
from jax.sharding import PartitionSpec as P

BOTH = ("row", "col")
XS, YS, ZS, CORES = 4, 4, 8, 2
UNIT = 16
STEP_K = 1024


def index_of(x, y, z, core):
    return ((y // 2) * ZS + z) * 16 + x * 4 + (y % 2) * 2 + core


def moved(values, target):
    pairs = []
    for place in np.ndindex(XS, YS, ZS, CORES):
        x, y, z, core = target(*place)
        pairs.append((index_of(*place), index_of(x % XS, y % YS, z % ZS, core)))
    return lax.ppermute(values, BOTH, pairs)


def ahead(x, y, z, core):
    return x, y, z + 1 - 2 * core, core


def behind(x, y, z, core):
    return x, y, z - 1 + 2 * core, core


def across(x, y, z, core):
    return x, y + 2, z, core


def other_core(x, y, z, core):
    return x, y, z, 1 - core


def along(sign):
    return ahead if sign > 0 else behind


def both(k, units):
    return tuple((s, u) for u in units for s in (k, -k))


GROUPS = (
    tuple((0, u) for u in "ABPQ") + both(1, "ABPQ"),
    both(2, "ABPQ"),
    both(3, "ABPQ") + tuple((4, u) for u in "ABPQ"),
)
CROSSINGS = ((0,), (1, -1), (2, -2), (3, -3), (4,))


def place_of(k, unit):
    if unit == "Q":
        group = next(g for g in CROSSINGS if k in g)
        return ("Q", group), UNIT * group.index(k)
    if unit in "AB" and abs(k) < 2:
        return ("S", k), UNIT * (unit == "B")
    if unit in "AP" and abs(k) > 1:
        return ("AP", k), UNIT * (unit == "P")
    return (unit, k), 0


def product_kernel(slots, arrays, held, before, last, core_ref, cov_ref, *refs):
    blocks = dict(zip(arrays, refs))
    total = refs[-1]
    core = core_ref[0]
    for at in range(0, cov_ref.shape[1], STEP_K):
        here = pl.ds(at, STEP_K)
        rows = []
        for k, unit in slots:
            name, first = place_of(k, unit)
            block = blocks[name][pl.ds(first, UNIT), here]
            if k not in (0, 4):
                name, first = place_of(-k, unit)
                block = jnp.where(core == 0, block, blocks[name][pl.ds(first, UNIT), here])
            rows.append(block)
        part = lax.dot_general(
            cov_ref[:, here], jnp.concatenate(rows, 0), (((1,), (1,)), ((), ())),
            preferred_element_type=jnp.float32,
        )
        total[...] = part if at == 0 else total[...] + part
    if last:
        earlier_ref, keep_ref, send_ref = refs[len(arrays) : len(arrays) + 3]
        for n in range(8):
            here = pl.ds(n * 32, 32)
            for out_ref, at in ((keep_ref, (2 * n + core) * 32), (send_ref, (2 * n + 1 - core) * 32)):
                out_ref[here, :before] = earlier_ref[pl.ds(at, 32), :]
                out_ref[here, before:] = total[pl.ds(at, 32), :]
    else:
        out_ref = refs[-2 - held]
        if before:
            out_ref[:, :before] = refs[len(arrays) + held][...]
        out_ref[:, before:] = total[...]


def in_vmem(values):
    return pltpu.with_memory_space_constraint(values, pltpu.VMEM)


def product(core, covariance, group, got, held, earlier=None):
    height, depth = covariance.shape
    slots, last = GROUPS[group], group == len(GROUPS) - 1
    before = 0 if earlier is None else earlier.shape[1]
    width = UNIT * len(slots)
    arrays = list(dict.fromkeys(place_of(*slot)[0] for slot in slots))
    vmem, as_is = pl.BlockSpec(memory_space=pltpu.VMEM), pl.BlockSpec(memory_space=pl.ANY)
    outs = 1 + last
    return pl.pallas_call(
        functools.partial(product_kernel, slots, arrays, len(held), before, last),
        in_specs=[pl.BlockSpec(memory_space=pltpu.SMEM), vmem]
        + [vmem] * len(arrays) + [as_is] * len(held) + [vmem] * (before > 0),
        out_specs=[vmem] * outs + [as_is] * len(held),
        out_shape=[jax.ShapeDtypeStruct((height // outs, before + width), jnp.float32)] * outs
        + [jax.ShapeDtypeStruct(h.shape, h.dtype) for h in held],
        input_output_aliases={2 + len(arrays) + n: outs + n for n in range(len(held))},
        scratch_shapes=[pltpu.VMEM((height, width), jnp.float32)],
        compiler_params=pltpu.CompilerParams(vmem_limit_bytes=6 * 1024 * 1024),
        cost_estimate=pl.CostEstimate(
            flops=2 * height * width * depth,
            bytes_accessed=2 * depth * (height + width),
            transcendentals=0,
        ),
    )(
        core, covariance, *(in_vmem(got[a]) for a in arrays), *held,
        *([in_vmem(earlier)] if before else []),
    )


def on_device(covariance, operator_rows, row_index):
    row, col = lax.axis_index("row"), lax.axis_index("col")
    core_of = jnp.full((1,), col % 2, jnp.int32)
    resident = in_vmem(covariance)
    got = {("S", 0): operator_rows}

    def send(unit, k):
        for sign in (1, -1) if k < 3 else (1,):
            got[unit, sign * (k + 1)] = moved(got[unit, sign * k], along(sign))

    def split(k):
        for step in sorted({k, -k}):
            got["A", step], got["B", step] = got["S", step][:UNIT], got["S", step][UNIT:]

    def rows_across(n):
        return jnp.concatenate([got["B", k] for k in CROSSINGS[n]], 0)

    def send_across(n, rows):
        got["Q", CROSSINGS[n]] = moved(rows, across)

    split(0)
    send("S", 0)
    got["P", 0] = moved(got["A", 0], across)
    send_across(0, rows_across(0))
    send("P", 0)
    split(1)
    send("B", 1)
    send_across(1, rows_across(1))
    for s in (1, -1):
        got["AP", s] = jnp.concatenate([got["A", s], got["P", s]], 0)
    send("AP", 1)
    send("B", 2)
    send_across(2, rows_across(2))
    send("AP", 2)
    send("B", 3)
    some, rows = product(core_of, resident, 0, got, [rows_across(3)])
    send_across(3, rows)
    most, rows = product(core_of, resident, 1, got, [rows_across(4)], some)
    send_across(4, rows)
    send("AP", 3)
    keep, sent = product(core_of, resident, 2, got, [], most)

    came = moved(sent, other_core)
    sums = (keep + came).reshape(8, 32, keep.shape[1])
    groups = [[2 * n + c for n in range(8)] for c in range(2)]
    apart = lax.all_to_all(sums, "col", 0, 0, axis_index_groups=groups)
    summed = apart.sum(0).astype(jnp.bfloat16)

    slots = [s for g in GROUPS for s in g]
    shift = np.repeat([-k for k, _ in slots], UNIT)
    far = np.repeat([u in "PQ" for _, u in slots], UNIT).astype(np.int32)
    first = np.repeat([UNIT * (u in "BQ") for _, u in slots], UNIT) + np.tile(np.arange(UNIT), len(slots))
    y_hi, z = row // ZS, row % ZS
    stored = (((y_hi + far) % 2) * ZS + (z + shift) % ZS) * (2 * UNIT) + first
    places = (stored[:, None] == row_index[None, :]).astype(jnp.bfloat16)
    ordered = jnp.dot(summed, places, preferred_element_type=jnp.float32)
    return ordered.astype(jnp.bfloat16)


def solution(mesh):
    in_specs = (P("row", "col"), P("row", "col"), P())
    out_specs = P(BOTH, None)
    return jax.shard_map(on_device, mesh=mesh, in_specs=in_specs, out_specs=out_specs, check_vma=False)
```

```python
import functools

import jax
import jax.numpy as jnp
import numpy as np
from jax import lax
from jax.experimental import pallas as pl
from jax.experimental.pallas import tpu as pltpu
from jax.sharding import PartitionSpec as P

BOTH = ("row", "col")
XS, YS, ZS, CORES = 4, 4, 8, 2
UNIT = 16
STEP_K = 1024


def index_of(x, y, z, core):
    return ((y // 2) * ZS + z) * 16 + x * 4 + (y % 2) * 2 + core


def moved(values, target):
    pairs = []
    for place in np.ndindex(XS, YS, ZS, CORES):
        x, y, z, core = target(*place)
        pairs.append((index_of(*place), index_of(x % XS, y % YS, z % ZS, core)))
    return lax.ppermute(values, BOTH, pairs)


def ahead(x, y, z, core):
    return x, y, z + 1 - 2 * core, core


def behind(x, y, z, core):
    return x, y, z - 1 + 2 * core, core


def across(x, y, z, core):
    return x, y + 2, z, core


def other_core(x, y, z, core):
    return x, y, z, 1 - core


def along(sign):
    return ahead if sign > 0 else behind


def both(k, units):
    return tuple((s, u) for u in units for s in (k, -k))


GROUPS = (
    tuple((0, u) for u in "ABPQ") + both(1, "ABPQ"),
    both(2, "ABPQ"),
    both(3, "ABPQ") + tuple((4, u) for u in "ABPQ"),
)
CROSSINGS = ((0,), (1, -1), (2, -2), (3, -3), (4,))


def place_of(k, unit):
    if unit == "Q":
        group = next(g for g in CROSSINGS if k in g)
        return ("Q", group), UNIT * group.index(k)
    return (unit, k), 0


def product_kernel(slots, arrays, held, before, last, core_ref, cov_ref, *refs):
    blocks = dict(zip(arrays, refs))
    total = refs[-1]
    core = core_ref[0]
    for at in range(0, cov_ref.shape[1], STEP_K):
        here = pl.ds(at, STEP_K)
        rows = []
        for k, unit in slots:
            name, first = place_of(k, unit)
            block = blocks[name][pl.ds(first, UNIT), here]
            if k not in (0, 4):
                name, first = place_of(-k, unit)
                block = jnp.where(core == 0, block, blocks[name][pl.ds(first, UNIT), here])
            rows.append(block)
        part = lax.dot_general(
            cov_ref[:, here], jnp.concatenate(rows, 0), (((1,), (1,)), ((), ())),
            preferred_element_type=jnp.float32,
        )
        total[...] = part if at == 0 else total[...] + part
    if last:
        earlier_ref, keep_ref, send_ref = refs[len(arrays) : len(arrays) + 3]
        for n in range(8):
            here = pl.ds(n * 32, 32)
            for out_ref, at in ((keep_ref, (2 * n + core) * 32), (send_ref, (2 * n + 1 - core) * 32)):
                out_ref[here, :before] = earlier_ref[pl.ds(at, 32), :]
                out_ref[here, before:] = total[pl.ds(at, 32), :]
    else:
        out_ref = refs[-2 - held]
        if before:
            out_ref[:, :before] = refs[len(arrays) + held][...]
        out_ref[:, before:] = total[...]


def in_vmem(values):
    return pltpu.with_memory_space_constraint(values, pltpu.VMEM)


def product(core, covariance, group, got, held, earlier=None):
    height, depth = covariance.shape
    slots, last = GROUPS[group], group == len(GROUPS) - 1
    before = 0 if earlier is None else earlier.shape[1]
    width = UNIT * len(slots)
    arrays = list(dict.fromkeys(place_of(*slot)[0] for slot in slots))
    vmem, as_is = pl.BlockSpec(memory_space=pltpu.VMEM), pl.BlockSpec(memory_space=pl.ANY)
    outs = 1 + last
    return pl.pallas_call(
        functools.partial(product_kernel, slots, arrays, len(held), before, last),
        in_specs=[pl.BlockSpec(memory_space=pltpu.SMEM), vmem]
        + [vmem] * len(arrays) + [as_is] * len(held) + [vmem] * (before > 0),
        out_specs=[vmem] * outs + [as_is] * len(held),
        out_shape=[jax.ShapeDtypeStruct((height // outs, before + width), jnp.float32)] * outs
        + [jax.ShapeDtypeStruct(h.shape, h.dtype) for h in held],
        input_output_aliases={2 + len(arrays) + n: outs + n for n in range(len(held))},
        scratch_shapes=[pltpu.VMEM((height, width), jnp.float32)],
        compiler_params=pltpu.CompilerParams(vmem_limit_bytes=24 * 1024 * 1024),
        cost_estimate=pl.CostEstimate(
            flops=2 * height * width * depth,
            bytes_accessed=2 * depth * (height + width),
            transcendentals=0,
        ),
    )(
        core, covariance, *(in_vmem(got[a]) for a in arrays), *held,
        *([in_vmem(earlier)] if before else []),
    )


def after(resident, values):
    return pl.pallas_call(
        lambda resident_ref, values_ref, out_ref: None,
        in_specs=[pl.BlockSpec(memory_space=pltpu.VMEM), pl.BlockSpec(memory_space=pl.ANY)],
        out_specs=pl.BlockSpec(memory_space=pl.ANY),
        out_shape=jax.ShapeDtypeStruct(values.shape, values.dtype),
        input_output_aliases={1: 0},
        compiler_params=pltpu.CompilerParams(vmem_limit_bytes=24 * 1024 * 1024),
    )(resident, values)


def on_device(covariance, operator_rows, row_index):
    row, col = lax.axis_index("row"), lax.axis_index("col")
    core_of = jnp.full((1,), col % 2, jnp.int32)
    resident = in_vmem(covariance)
    got = {("S", 0): operator_rows}

    def send(unit, k):
        for sign in (1, -1) if k < 3 else (1,):
            got[unit, sign * (k + 1)] = moved(got[unit, sign * k], along(sign))

    def split(k):
        for step in sorted({k, -k}):
            got["A", step], got["B", step] = got["S", step][:UNIT], got["S", step][UNIT:]

    def rows_across(n):
        return jnp.concatenate([got["B", k] for k in CROSSINGS[n]], 0)

    def send_across(n, rows):
        got["Q", CROSSINGS[n]] = moved(rows, across)

    split(0)
    got["P", 0] = moved(got["A", 0], across)
    send("B", 0)
    send("A", 0)
    send_across(0, after(resident, rows_across(0)))
    send("B", 1)
    send("P", 0)
    send_across(1, rows_across(1))
    send("A", 1)
    send("B", 2)
    send("P", 1)
    send_across(2, rows_across(2))
    some, got["A", 2], got["A", -2] = product(core_of, resident, 0, got, [got["A", 2], got["A", -2]])
    send("A", 2)
    send("B", 3)
    send("P", 2)
    send_across(3, rows_across(3))
    send_across(4, rows_across(4))
    most, got["A", 3] = product(core_of, resident, 1, got, [got["A", 3]], some)
    send("A", 3)
    send("P", 3)
    keep, sent = product(core_of, resident, 2, got, [], most)

    came = moved(sent, other_core)
    sums = (keep + came).reshape(8, 32, keep.shape[1])
    groups = [[2 * n + c for n in range(8)] for c in range(2)]
    apart = lax.all_to_all(sums, "col", 0, 0, axis_index_groups=groups)
    summed = apart.sum(0).astype(jnp.bfloat16)

    slots = [s for g in GROUPS for s in g]
    shift = np.repeat([-k for k, _ in slots], UNIT)
    far = np.repeat([u in "PQ" for _, u in slots], UNIT).astype(np.int32)
    first = np.repeat([UNIT * (u in "BQ") for _, u in slots], UNIT) + np.tile(np.arange(UNIT), len(slots))
    y_hi, z = row // ZS, row % ZS
    stored = (((y_hi + far) % 2) * ZS + (z + shift) % ZS) * (2 * UNIT) + first
    places = (stored[:, None] == row_index[None, :]).astype(jnp.bfloat16)
    ordered = jnp.dot(summed, places, preferred_element_type=jnp.float32)
    return ordered.astype(jnp.bfloat16)


def solution(mesh):
    in_specs = (P("row", "col"), P("row", "col"), P())
    out_specs = P(BOTH, None)
    return jax.shard_map(on_device, mesh=mesh, in_specs=in_specs, out_specs=out_specs, check_vma=False)
```

```python
import functools

import jax
import jax.numpy as jnp
import numpy as np
from jax import lax
from jax.experimental import pallas as pl
from jax.experimental.pallas import tpu as pltpu
from jax.sharding import PartitionSpec as P

BOTH = ("row", "col")
XS, YS, ZS, CORES = 4, 4, 8, 2
UNIT = 16
STEP_K = 1024


def index_of(x, y, z, core):
    return ((y // 2) * ZS + z) * 16 + x * 4 + (y % 2) * 2 + core


def moved(values, target):
    pairs = []
    for place in np.ndindex(XS, YS, ZS, CORES):
        x, y, z, core = target(*place)
        pairs.append((index_of(*place), index_of(x % XS, y % YS, z % ZS, core)))
    return lax.ppermute(values, BOTH, pairs)


def ahead(x, y, z, core):
    return x, y, z + 1 - 2 * core, core


def behind(x, y, z, core):
    return x, y, z - 1 + 2 * core, core


def across(x, y, z, core):
    return x, y + 2, z, core


def other_core(x, y, z, core):
    return x, y, z, 1 - core


def along(sign):
    return ahead if sign > 0 else behind


def both(k, units):
    return tuple((s, u) for u in units for s in (k, -k))


GROUPS = (
    tuple((0, u) for u in "ABPQ") + both(1, "ABPQ") + both(2, "AB"),
    both(2, "PQ") + both(3, "ABPQ") + tuple((4, u) for u in "ABPQ"),
)
CROSSINGS = ((0,), (1, -1), (2, -2), (3, -3), (4,))


def place_of(k, unit):
    if unit == "Q":
        group = next(g for g in CROSSINGS if k in g)
        return ("Q", group), UNIT * group.index(k)
    return (unit, k), 0


def product_kernel(slots, arrays, held, before, last, core_ref, cov_ref, *refs):
    blocks = dict(zip(arrays, refs))
    total = refs[-1]
    core = core_ref[0]
    for at in range(0, cov_ref.shape[1], STEP_K):
        here = pl.ds(at, STEP_K)
        rows = []
        for k, unit in slots:
            name, first = place_of(k, unit)
            block = blocks[name][pl.ds(first, UNIT), here]
            if k not in (0, 4):
                name, first = place_of(-k, unit)
                block = jnp.where(core == 0, block, blocks[name][pl.ds(first, UNIT), here])
            rows.append(block)
        part = lax.dot_general(
            cov_ref[:, here], jnp.concatenate(rows, 0), (((1,), (1,)), ((), ())),
            preferred_element_type=jnp.float32,
        )
        total[...] = part if at == 0 else total[...] + part
    if last:
        earlier_ref, keep_ref, send_ref = refs[len(arrays) : len(arrays) + 3]
        for n in range(8):
            here = pl.ds(n * 32, 32)
            for out_ref, at in ((keep_ref, (2 * n + core) * 32), (send_ref, (2 * n + 1 - core) * 32)):
                out_ref[here, :before] = earlier_ref[pl.ds(at, 32), :]
                out_ref[here, before:] = total[pl.ds(at, 32), :]
    else:
        out_ref = refs[-2 - held]
        if before:
            out_ref[:, :before] = refs[len(arrays) + held][...]
        out_ref[:, before:] = total[...]


def in_vmem(values):
    return pltpu.with_memory_space_constraint(values, pltpu.VMEM)


def product(core, covariance, group, got, held, earlier=None):
    height, depth = covariance.shape
    slots, last = GROUPS[group], group == len(GROUPS) - 1
    before = 0 if earlier is None else earlier.shape[1]
    width = UNIT * len(slots)
    arrays = list(dict.fromkeys(place_of(*slot)[0] for slot in slots))
    vmem, as_is = pl.BlockSpec(memory_space=pltpu.VMEM), pl.BlockSpec(memory_space=pl.ANY)
    outs = 1 + last
    return pl.pallas_call(
        functools.partial(product_kernel, slots, arrays, len(held), before, last),
        in_specs=[pl.BlockSpec(memory_space=pltpu.SMEM), vmem]
        + [vmem] * len(arrays) + [as_is] * len(held) + [vmem] * (before > 0),
        out_specs=[vmem] * outs + [as_is] * len(held),
        out_shape=[jax.ShapeDtypeStruct((height // outs, before + width), jnp.float32)] * outs
        + [jax.ShapeDtypeStruct(h.shape, h.dtype) for h in held],
        input_output_aliases={2 + len(arrays) + n: outs + n for n in range(len(held))},
        scratch_shapes=[pltpu.VMEM((height, width), jnp.float32)],
        compiler_params=pltpu.CompilerParams(vmem_limit_bytes=24 * 1024 * 1024),
        cost_estimate=pl.CostEstimate(
            flops=2 * height * width * depth,
            bytes_accessed=2 * depth * (height + width),
            transcendentals=0,
        ),
    )(
        core, covariance, *(in_vmem(got[a]) for a in arrays), *held,
        *([in_vmem(earlier)] if before else []),
    )


def after(resident, values):
    return pl.pallas_call(
        lambda resident_ref, values_ref, out_ref: None,
        in_specs=[pl.BlockSpec(memory_space=pltpu.VMEM), pl.BlockSpec(memory_space=pl.ANY)],
        out_specs=pl.BlockSpec(memory_space=pl.ANY),
        out_shape=jax.ShapeDtypeStruct(values.shape, values.dtype),
        input_output_aliases={1: 0},
        compiler_params=pltpu.CompilerParams(vmem_limit_bytes=24 * 1024 * 1024),
    )(resident, values)


def on_device(covariance, operator_rows, row_index):
    row, col = lax.axis_index("row"), lax.axis_index("col")
    core_of = jnp.full((1,), col % 2, jnp.int32)
    resident = in_vmem(covariance)
    got = {("S", 0): operator_rows}

    def send(unit, k):
        for sign in (1, -1) if k < 3 else (1,):
            got[unit, sign * (k + 1)] = moved(got[unit, sign * k], along(sign))

    def split(k):
        for step in sorted({k, -k}):
            got["A", step], got["B", step] = got["S", step][:UNIT], got["S", step][UNIT:]

    def rows_across(n):
        return jnp.concatenate([got["B", k] for k in CROSSINGS[n]], 0)

    def send_across(n, rows):
        got["Q", CROSSINGS[n]] = moved(rows, across)

    split(0)
    got["P", 0] = moved(got["A", 0], across)
    send("B", 0)
    send("A", 0)
    send_across(0, after(resident, rows_across(0)))
    send("B", 1)
    send("P", 0)
    send_across(1, rows_across(1))
    send("A", 1)
    send("B", 2)
    send("P", 1)
    send_across(2, rows_across(2))
    send("A", 2)
    some, got["P", 2], got["P", -2] = product(core_of, resident, 0, got, [got["P", 2], got["P", -2]])
    send("B", 3)
    send("P", 2)
    send_across(3, rows_across(3))
    send_across(4, rows_across(4))
    send("A", 3)
    send("P", 3)
    keep, sent = product(core_of, resident, 1, got, [], some)

    came = moved(sent, other_core)
    sums = (keep + came).reshape(8, 32, keep.shape[1])
    groups = [[2 * n + c for n in range(8)] for c in range(2)]
    apart = lax.all_to_all(sums, "col", 0, 0, axis_index_groups=groups)
    summed = apart.sum(0).astype(jnp.bfloat16)

    slots = [s for g in GROUPS for s in g]
    shift = np.repeat([-k for k, _ in slots], UNIT)
    far = np.repeat([u in "PQ" for _, u in slots], UNIT).astype(np.int32)
    first = np.repeat([UNIT * (u in "BQ") for _, u in slots], UNIT) + np.tile(np.arange(UNIT), len(slots))
    y_hi, z = row // ZS, row % ZS
    stored = (((y_hi + far) % 2) * ZS + (z + shift) % ZS) * (2 * UNIT) + first
    places = (stored[:, None] == row_index[None, :]).astype(jnp.bfloat16)
    ordered = jnp.dot(summed, places, preferred_element_type=jnp.float32)
    return ordered.astype(jnp.bfloat16)


def solution(mesh):
    in_specs = (P("row", "col"), P("row", "col"), P())
    out_specs = P(BOTH, None)
    return jax.shard_map(on_device, mesh=mesh, in_specs=in_specs, out_specs=out_specs, check_vma=False)
```

```python
import functools

import jax
import jax.numpy as jnp
import numpy as np
from jax import lax
from jax.experimental import pallas as pl
from jax.experimental.pallas import tpu as pltpu
from jax.sharding import PartitionSpec as P

BOTH = ("row", "col")
XS, YS, ZS, CORES = 4, 4, 8, 2
UNIT = 16
STEP_K = 1024


def index_of(x, y, z, core):
    return ((y // 2) * ZS + z) * 16 + x * 4 + (y % 2) * 2 + core


def moved(values, target):
    pairs = []
    for place in np.ndindex(XS, YS, ZS, CORES):
        x, y, z, core = target(*place)
        pairs.append((index_of(*place), index_of(x % XS, y % YS, z % ZS, core)))
    return lax.ppermute(values, BOTH, pairs)


def ahead(x, y, z, core):
    return x, y, z + 1 - 2 * core, core


def behind(x, y, z, core):
    return x, y, z - 1 + 2 * core, core


def across(x, y, z, core):
    return x, y + 2, z, core


def other_core(x, y, z, core):
    return x, y, z, 1 - core


def along(sign):
    return ahead if sign > 0 else behind


def both(k, units):
    return tuple((s, u) for u in units for s in (k, -k))


GROUPS = (
    tuple((0, u) for u in "ABPQ") + both(1, "ABPQ"),
    both(2, "ABPQ"),
    both(3, "ABPQ") + tuple((4, u) for u in "ABPQ"),
)
CROSSINGS = ((0,), (1, -1), (2, -2), (3, -3), (4,))


def place_of(k, unit):
    if unit == "Q":
        group = next(g for g in CROSSINGS if k in g)
        return ("Q", group), UNIT * group.index(k)
    return (unit, k), 0


def product_kernel(slots, arrays, held, before, last, core_ref, cov_ref, *refs):
    blocks = dict(zip(arrays, refs))
    total = refs[-1]
    core = core_ref[0]
    for at in range(0, cov_ref.shape[1], STEP_K):
        here = pl.ds(at, STEP_K)
        rows = []
        for k, unit in slots:
            name, first = place_of(k, unit)
            block = blocks[name][pl.ds(first, UNIT), here]
            if k not in (0, 4):
                name, first = place_of(-k, unit)
                block = jnp.where(core == 0, block, blocks[name][pl.ds(first, UNIT), here])
            rows.append(block)
        part = lax.dot_general(
            cov_ref[:, here], jnp.concatenate(rows, 0), (((1,), (1,)), ((), ())),
            preferred_element_type=jnp.float32,
        )
        total[...] = part if at == 0 else total[...] + part
    if last:
        earlier_ref, keep_ref, send_ref = refs[len(arrays) : len(arrays) + 3]
        for n in range(8):
            here = pl.ds(n * 32, 32)
            for out_ref, at in ((keep_ref, (2 * n + core) * 32), (send_ref, (2 * n + 1 - core) * 32)):
                out_ref[here, :before] = earlier_ref[pl.ds(at, 32), :]
                out_ref[here, before:] = total[pl.ds(at, 32), :]
    else:
        out_ref = refs[-2 - held]
        if before:
            out_ref[:, :before] = refs[len(arrays) + held][...]
        out_ref[:, before:] = total[...]


def in_vmem(values):
    return pltpu.with_memory_space_constraint(values, pltpu.VMEM)


def product(core, covariance, group, got, held, earlier=None):
    height, depth = covariance.shape
    slots, last = GROUPS[group], group == len(GROUPS) - 1
    before = 0 if earlier is None else earlier.shape[1]
    width = UNIT * len(slots)
    arrays = list(dict.fromkeys(place_of(*slot)[0] for slot in slots))
    vmem, as_is = pl.BlockSpec(memory_space=pltpu.VMEM), pl.BlockSpec(memory_space=pl.ANY)
    outs = 1 + last
    return pl.pallas_call(
        functools.partial(product_kernel, slots, arrays, len(held), before, last),
        in_specs=[pl.BlockSpec(memory_space=pltpu.SMEM), vmem]
        + [vmem] * len(arrays) + [as_is] * len(held) + [vmem] * (before > 0),
        out_specs=[vmem] * outs + [as_is] * len(held),
        out_shape=[jax.ShapeDtypeStruct((height // outs, before + width), jnp.float32)] * outs
        + [jax.ShapeDtypeStruct(h.shape, h.dtype) for h in held],
        input_output_aliases={2 + len(arrays) + n: outs + n for n in range(len(held))},
        scratch_shapes=[pltpu.VMEM((height, width), jnp.float32)],
        compiler_params=pltpu.CompilerParams(vmem_limit_bytes=24 * 1024 * 1024),
        cost_estimate=pl.CostEstimate(
            flops=2 * height * width * depth,
            bytes_accessed=2 * depth * (height + width),
            transcendentals=0,
        ),
    )(
        core, covariance, *(in_vmem(got[a]) for a in arrays), *held,
        *([in_vmem(earlier)] if before else []),
    )


def after(resident, values):
    return pl.pallas_call(
        lambda resident_ref, values_ref, out_ref: None,
        in_specs=[pl.BlockSpec(memory_space=pltpu.VMEM), pl.BlockSpec(memory_space=pl.ANY)],
        out_specs=pl.BlockSpec(memory_space=pl.ANY),
        out_shape=jax.ShapeDtypeStruct(values.shape, values.dtype),
        input_output_aliases={1: 0},
        compiler_params=pltpu.CompilerParams(vmem_limit_bytes=24 * 1024 * 1024),
    )(resident, values)


def on_device(covariance, operator_rows, row_index):
    row, col = lax.axis_index("row"), lax.axis_index("col")
    core_of = jnp.full((1,), col % 2, jnp.int32)
    resident = in_vmem(covariance)
    got = {("S", 0): operator_rows}

    def send(unit, k):
        for sign in (1, -1) if k < 3 else (1,):
            got[unit, sign * (k + 1)] = moved(got[unit, sign * k], along(sign))

    def split(k):
        for step in sorted({k, -k}):
            got["A", step], got["B", step] = got["S", step][:UNIT], got["S", step][UNIT:]

    def rows_across(n):
        return jnp.concatenate([got["B", k] for k in CROSSINGS[n]], 0)

    def send_across(n, rows):
        got["Q", CROSSINGS[n]] = moved(rows, across)

    split(0)
    got["P", 0] = moved(got["A", 0], across)
    send("B", 0)
    send("A", 0)
    send_across(0, after(resident, rows_across(0)))
    send("B", 1)
    send("P", 0)
    send_across(1, rows_across(1))
    send("A", 1)
    send("B", 2)
    send("P", 1)
    send_across(2, rows_across(2))
    some, got["B", 3], got["B", -3] = product(core_of, resident, 0, got, [got["B", 3], got["B", -3]])
    send("B", 3)
    send("P", 2)
    send("A", 2)
    send_across(3, rows_across(3))
    send_across(4, rows_across(4))
    most, got["A", 3] = product(core_of, resident, 1, got, [got["A", 3]], some)
    send("A", 3)
    send("P", 3)
    keep, sent = product(core_of, resident, 2, got, [], most)

    came = moved(sent, other_core)
    sums = (keep + came).reshape(8, 32, keep.shape[1])
    groups = [[2 * n + c for n in range(8)] for c in range(2)]
    apart = lax.all_to_all(sums, "col", 0, 0, axis_index_groups=groups)
    summed = apart.sum(0).astype(jnp.bfloat16)

    slots = [s for g in GROUPS for s in g]
    shift = np.repeat([-k for k, _ in slots], UNIT)
    far = np.repeat([u in "PQ" for _, u in slots], UNIT).astype(np.int32)
    first = np.repeat([UNIT * (u in "BQ") for _, u in slots], UNIT) + np.tile(np.arange(UNIT), len(slots))
    y_hi, z = row // ZS, row % ZS
    stored = (((y_hi + far) % 2) * ZS + (z + shift) % ZS) * (2 * UNIT) + first
    places = (stored[:, None] == row_index[None, :]).astype(jnp.bfloat16)
    ordered = jnp.dot(summed, places, preferred_element_type=jnp.float32)
    return ordered.astype(jnp.bfloat16)


def solution(mesh):
    in_specs = (P("row", "col"), P("row", "col"), P())
    out_specs = P(BOTH, None)
    return jax.shard_map(on_device, mesh=mesh, in_specs=in_specs, out_specs=out_specs, check_vma=False)
```
